32 devices in a mesh: exam: 2 (over x), slab: 16 (over z, y, core).
Axes of the slice: x: 2, y: 2, z: 4, core: 2. Of those that a mesh axis runs over, the one named last changes fastest.
Arguments:
- measured: bfloat16 [4, 16, 128, 16, 320], P('exam', None, None, 'slab'), parts along dimension 0, may hold values from -6 to 6
- coil_maps: bfloat16 [4, 16, 128, 16, 320], P('exam', None, 'slab'), parts along dimension 0, may hold values from -2.5 to 2.5
- start_image: float32 [4, 128, 16, 320], P('exam', 'slab'), parts along dimension 0, may hold values from -6 to 6
- line_mask: int32 [256, 320], P('exam'), parts along dimension 0, may hold values 0 or 1
- conv_plane: bfloat16 [32, 2, 3, 3], replicated, may hold values from -1.5 to 1.5
- conv_depth: bfloat16 [32, 3, 32], replicated, may hold values from -0.625 to 0.625
- conv_output: bfloat16 [2, 32], replicated, may hold values from -1 to 1
Outputs:
- final_image: float32 [4, 128, 16, 320], P('exam', 'slab'), parts along dimension 0
The draws below stay inside these ranges and needn't reach their ends.
There are 2 independent parts, one for each index of `exam`. The reference program is written for one: setup_inputs(seed, part) draws one part's arguments, and reference() takes and returns one part's arrays. A program takes and returns all parts, laid end to end along the dimension named above; an argument that names none is the same for every part. Nothing has to cross between parts.
All inputs are finite; a program needn't handle non-finite values.
Results may differ from the reference program's by a relative error of at most 0.015.
Values may be sent and summed in bfloat16 or wider, within the bound.
A program may use at most 128 MiB of HBM per device.

```python
import math
import jax
import jax.numpy as jnp
from jax import lax

C = 16
Y = 320
Z = 128
H = 32
PASSES = 2
X = 16


def place_ends(drawn, stream_key, smallest, high):
    longest = drawn.shape.index(max(drawn.shape))
    spots = []
    for shift in (0, 1):
        where = [jax.random.randint(jax.random.fold_in(stream_key, axis), (), 0, length) for axis, length in enumerate(drawn.shape)]
        where[longest] = (where[longest] + shift) % drawn.shape[longest]
        spots.append(tuple(where))
    return drawn.at[spots[0]].set(smallest).at[spots[1]].set(high)


def steps_of(key, dims, shards, smallest, high):
    loudness = 1.0
    for axis_at, parts in shards:
        heights = jax.random.uniform(jax.random.fold_in(jax.random.fold_in(key, 6), axis_at), (parts,), jnp.float32, smallest / len(shards), high / len(shards))
        loudness = loudness * jnp.repeat(jnp.exp(heights), dims[axis_at] // parts).reshape((-1,) + (1,) * (len(dims) - 1 - axis_at))
    return loudness


def bell_draw(key, extent, width, limit, split=(), kind=jnp.bfloat16):
    values = jax.random.normal(key, extent, jnp.float32) * width
    if len(split) > 0:
        values = steps_of(key, extent, split, -0.22, 0.18) * values
    return jnp.clip(values, min=-limit, max=limit).astype(kind)


def setup_inputs(seed: int = 0, part: int = 0) -> dict:
    seeds = jax.random.split(jax.random.key(seed), 8)
    part_splits = jax.random.split(jax.random.fold_in(seeds[7], part), 8)
    return {
        "measured": bell_draw(part_splits[0], (2, C, Z, X, Y), 1.0, 6.0, ((3, 16),)),
        "coil_maps": bell_draw(part_splits[1], (2, C, Z, X, Y), ((2 * C) ** -0.5), 2.5, ((2, 16),)),
        "start_image": bell_draw(part_splits[2], (2, Z, X, Y), 1.0, 6.0, ((1, 16),), jnp.float32),
        "line_mask": place_ends((jax.random.randint(part_splits[3], (Z, Y), 0, 3) < 1).astype(jnp.int32), jax.random.fold_in(part_splits[3], 1), 0, 1),
        "conv_plane": bell_draw(seeds[4], (H, 2, 3, 3), 18 ** -0.5, 1.5),
        "conv_depth": bell_draw(seeds[5], (H, 3, H), (3 * H) ** -0.5, 0.625),
        "conv_output": bell_draw(seeds[6], (2, H), H ** -0.5, 1.0),
    }


def dft_table(length):
    position = jnp.arange(length, dtype=jnp.int32)
    product_mod = position[:, None] * position[None, :] % length
    angles = product_mod.astype(jnp.float32) * (2.0 * math.pi / length)
    norm_scale = 1.0 / math.sqrt(length)
    cosine = jnp.cos(angles) * norm_scale
    sine = jnp.sin(angles) * norm_scale
    upper_half = jnp.stack([cosine, sine], axis=1)
    lower_half = jnp.stack([-sine, cosine], axis=1)
    return jnp.stack([upper_half, lower_half], axis=0).astype(jnp.bfloat16)

def round_low(values):
    return lax.optimization_barrier(values.astype(jnp.bfloat16)).astype(jnp.float32)

def complex_times(maps, values):
    return jnp.stack([maps[0] * values[0] - maps[1] * values[1], maps[0] * values[1] + maps[1] * values[0]])

def conj_times(maps, values):
    return jnp.stack([maps[0] * values[0] + maps[1] * values[1], maps[0] * values[1] - maps[1] * values[0]])

def denoise_ref(noisy_low, conv_plane, conv_depth, conv_output):
    highest = lax.Precision.HIGHEST
    first = lax.conv_general_dilated(noisy_low, conv_plane.astype(jnp.float32), (1, 1), 'SAME', dimension_numbers=('CNHW', 'OIHW', 'CNHW'), precision=highest)
    act_one = round_low(jax.nn.relu(first))
    planes = act_one.shape[1]
    padded = jnp.pad(act_one, ((0, 0), (1, 1), (0, 0), (0, 0)))
    depth = conv_depth.astype(jnp.float32)
    mixed = jnp.einsum('oi,izxy->ozxy', depth[:, 0, :], padded[:, 0:planes], precision=highest)
    for offset in range(1, 3):
        mixed = mixed + jnp.einsum('oi,izxy->ozxy', depth[:, offset, :], padded[:, offset:offset + planes], precision=highest)
    act_two = round_low(jax.nn.relu(mixed))
    return jnp.einsum('pi,izxy->pzxy', conv_output.astype(jnp.float32), act_two, precision=highest)

def reference(measured, coil_maps, start_image, line_mask, conv_plane, conv_depth, conv_output):
    highest = lax.Precision.HIGHEST
    table_y = dft_table(measured.shape[4]).astype(jnp.float32)
    table_z = dft_table(measured.shape[2]).astype(jnp.float32)
    sample_gate = line_mask.astype(jnp.float32)[:, None, :]
    maps_first = jnp.moveaxis(coil_maps, 1, 0)
    data_first = jnp.moveaxis(measured, 1, 0)
    estimate = start_image
    for index_pass in range(PASSES):
        image_low = round_low(estimate)

        def one_coil(gradient, inputs):
            maps = inputs[0].astype(jnp.float32)
            coil_image = round_low(complex_times(maps, image_low))
            hybrid = round_low(jnp.einsum('pkqn,qzxn->pzxk', table_y, coil_image, precision=highest))
            predicted = jnp.einsum('pkqn,qnxy->pkxy', table_z, hybrid, precision=highest)
            residual = round_low(sample_gate * (predicted - inputs[1].astype(jnp.float32)))
            back_z = round_low(jnp.einsum('qkpn,qkxy->pnxy', table_z, residual, precision=highest))
            back_y = jnp.einsum('qkpn,qzxk->pzxn', table_y, back_z, precision=highest)
            return (gradient + conj_times(maps, back_y), None)
        gradient, unused = lax.scan(one_coil, jnp.zeros_like(estimate), (maps_first, data_first))
        noisy_image = estimate - gradient
        estimate = noisy_image + denoise_ref(round_low(noisy_image), conv_plane, conv_depth, conv_output)
    return estimate
```

```python
import math

import jax
import jax.numpy as jnp
from jax import lax
from jax.sharding import PartitionSpec as P

PASSES = 2


def padded_2(array, sides, width):
    for axis, dim in sides:
        size, length = (lax.axis_size(axis), array.shape[dim])
        up = [(i, (i + 1) % size) for i in range(size - 1)]
        down = [(j, i) for i, j in up]
        last = lax.slice_in_dim(array, length - width, length, axis=dim)
        initial = lax.slice_in_dim(array, 0, width, axis=dim)
        before = lax.ppermute(last, axis, up)
        after = lax.ppermute(initial, axis, down)
        array = jnp.concatenate([before, array, after], axis=dim)
    return array


def dft_table(length):
    position = jnp.arange(length, dtype=jnp.int32)
    product_mod = position[:, None] * position[None, :] % length
    angles = product_mod.astype(jnp.float32) * (2.0 * math.pi / length)
    norm_scale = 1.0 / math.sqrt(length)
    cosine = jnp.cos(angles) * norm_scale
    sine = jnp.sin(angles) * norm_scale
    upper_half = jnp.stack([cosine, sine], axis=1)
    lower_half = jnp.stack([-sine, cosine], axis=1)
    return jnp.stack([upper_half, lower_half], axis=0).astype(jnp.bfloat16)


def complex_times(maps, values):
    maps_real = maps[0].astype(jnp.float32)
    maps_imag = maps[1].astype(jnp.float32)
    value_real = values[0].astype(jnp.float32)
    value_imag = values[1].astype(jnp.float32)
    return jnp.stack(
        [
            maps_real * value_real - maps_imag * value_imag,
            maps_real * value_imag + maps_imag * value_real,
        ]
    ).astype(jnp.bfloat16)


def conj_summed(maps, values):
    maps_real = maps[0].astype(jnp.float32)
    maps_imag = maps[1].astype(jnp.float32)
    real_part = jnp.sum(maps_real * values[0] + maps_imag * values[1], axis=0)
    imag_part = jnp.sum(maps_real * values[1] - maps_imag * values[0], axis=0)
    return jnp.stack([real_part, imag_part])


def forward_y(table_y, coil_image):
    return jnp.einsum(
        "pkqn,qcabn->pcabk", table_y, coil_image, preferred_element_type=jnp.float32
    ).astype(jnp.bfloat16)


def inverse_y(table_y, back_z):
    return jnp.einsum("qkpn,qcabk->pcabn", table_y, back_z, preferred_element_type=jnp.float32)


def residual_back(table_z, hybrid, measured, sample_gate):
    predicted = jnp.einsum("pkqn,qcnxy->pckxy", table_z, hybrid, preferred_element_type=jnp.float32)
    residual = (sample_gate * (predicted - measured.astype(jnp.float32))).astype(jnp.bfloat16)
    return jnp.einsum(
        "qkpn,qckxy->pcnxy", table_z, residual, preferred_element_type=jnp.float32
    ).astype(jnp.bfloat16)


def plane_conv(values, conv_plane):
    first = lax.conv_general_dilated(
        values,
        conv_plane,
        (1, 1),
        "SAME",
        dimension_numbers=("CNHW", "OIHW", "CNHW"),
        preferred_element_type=jnp.float32,
    )
    return jax.nn.relu(first).astype(jnp.bfloat16)


def denoise(noisy_low, conv_plane, conv_depth, conv_output):
    planes = noisy_low.shape[1]
    wide = padded_2(noisy_low, (("slab", 2),), 1)
    first = lax.conv_general_dilated(
        wide,
        conv_plane,
        (1, 1),
        ((0, 0), (1, 1)),
        dimension_numbers=("CNHW", "OIHW", "CNHW"),
        preferred_element_type=jnp.float32,
    )
    act_one = jax.nn.relu(first).astype(jnp.bfloat16)
    padded = jnp.pad(act_one, ((0, 0), (1, 1), (0, 0), (0, 0)))
    stacked = jnp.concatenate([padded[:, t : t + planes] for t in range(3)], axis=0)
    depth = conv_depth.reshape(conv_depth.shape[0], -1)
    mixed = jnp.einsum("oi,izxy->ozxy", depth, stacked, preferred_element_type=jnp.float32)
    act_two = jax.nn.relu(mixed).astype(jnp.bfloat16)
    return jnp.einsum("pi,izxy->pzxy", conv_output, act_two, preferred_element_type=jnp.float32)


def body(measured, coil_maps, start_image, line_mask, conv_plane, conv_depth, conv_output):
    table_y = dft_table(measured.shape[4])
    table_z = dft_table(measured.shape[2])
    sample_gate = line_mask.astype(jnp.float32)[:, None, :]
    sent = jnp.concatenate([coil_maps, start_image.astype(jnp.bfloat16)[:, None]], axis=1)
    got = lax.all_to_all(sent, "slab", split_axis=3, concat_axis=2, tiled=True)
    coils = coil_maps.shape[1]
    maps = got[:, :coils]
    estimate = got[:, coils].astype(jnp.float32)
    for index_pass in range(PASSES):
        image_low = estimate.astype(jnp.bfloat16)
        coil_image = complex_times(maps, image_low[:, None])
        hybrid = forward_y(table_y, coil_image)
        back_z = residual_back(table_z, hybrid, measured, sample_gate)
        back_y = inverse_y(table_y, back_z)
        gradient = conj_summed(maps, back_y)
        noisy_image = estimate - gradient
        estimate = noisy_image + denoise(
            noisy_image.astype(jnp.bfloat16), conv_plane, conv_depth, conv_output
        )
    out = lax.all_to_all(
        estimate.astype(jnp.bfloat16), "slab", split_axis=1, concat_axis=2, tiled=True
    )
    return out.astype(jnp.float32)


def solution(mesh):
    in_specs = (
        P("exam", None, None, "slab", None),
        P("exam", None, "slab", None, None),
        P("exam", "slab", None, None),
        P("exam", None),
        P(),
        P(),
        P(),
    )
    out_specs = P("exam", "slab", None, None)
    return jax.shard_map(body, mesh=mesh, in_specs=in_specs, out_specs=out_specs, check_vma=False)
```

```python
import functools
import math

import jax
import jax.numpy as jnp
from jax import lax
from jax.experimental import pallas as pl
from jax.experimental.pallas import tpu as pltpu
from jax.sharding import PartitionSpec as P

PASSES = 2


def partner(me, flips):
    other = me
    bit = 1
    while bit <= flips:
        if flips & bit:
            other = other + bit * (1 - 2 * lax.rem(lax.div(me, bit), 2))
        bit *= 2
    return other


def flip_order(size):
    half = size // 2
    order = []
    for low in range(half):
        order.append(half + low)
        if low:
            order.append(low)
    return order


def exchange_kernel(size, sent_ref, got_ref, send_sem, recv_sem, own_sem):
    me = lax.axis_index("slab")
    order = flip_order(size)
    barrier = pltpu.get_barrier_semaphore()
    for flips in order:
        pl.semaphore_signal(barrier, inc=1, device_id={"slab": partner(me, flips)})
    own = pltpu.make_async_copy(sent_ref.at[me], got_ref.at[me], own_sem)
    own.start()
    pl.semaphore_wait(barrier, size - 1)
    copies = []
    for flips in order:
        to = partner(me, flips)
        copy = pltpu.make_async_remote_copy(
            src_ref=sent_ref.at[to],
            dst_ref=got_ref.at[me],
            send_sem=send_sem.at[flips],
            recv_sem=recv_sem.at[flips],
            device_id={"slab": to},
        )
        copy.start()
        copies.append(copy)
    own.wait()
    for copy in copies:
        copy.wait()


def exchange(blocks, identity, space):
    size = blocks.shape[0]
    return pl.pallas_call(
        functools.partial(exchange_kernel, size),
        out_shape=jax.ShapeDtypeStruct(blocks.shape, blocks.dtype),
        in_specs=[pl.BlockSpec(memory_space=space)],
        out_specs=pl.BlockSpec(memory_space=space),
        scratch_shapes=[
            pltpu.SemaphoreType.DMA((size,)),
            pltpu.SemaphoreType.DMA((size,)),
            pltpu.SemaphoreType.DMA,
        ],
        compiler_params=pltpu.CompilerParams(
            collective_id=identity, has_side_effects=True, vmem_limit_bytes=32 << 20
        ),
    )(blocks)


def halo_kernel(size, plane_ref, out_ref, send_sem, recv_sem):
    me = lax.axis_index("slab")
    sides = (lax.rem(me + 1, size), lax.rem(me + size - 1, size))
    barrier = pltpu.get_barrier_semaphore()
    for side in sides:
        pl.semaphore_signal(barrier, inc=1, device_id={"slab": side})
    pl.semaphore_wait(barrier, 2)
    copies = []
    for at, side in enumerate(sides):
        copy = pltpu.make_async_remote_copy(
            src_ref=plane_ref,
            dst_ref=out_ref.at[at],
            send_sem=send_sem.at[at],
            recv_sem=recv_sem.at[at],
            device_id={"slab": side},
        )
        copy.start()
        copies.append(copy)
    for copy in copies:
        copy.wait()


def halos(plane, identity):
    size = lax.axis_size("slab")
    me = lax.axis_index("slab")
    got = pl.pallas_call(
        functools.partial(halo_kernel, size),
        out_shape=jax.ShapeDtypeStruct((2,) + plane.shape, plane.dtype),
        in_specs=[pl.BlockSpec(memory_space=pltpu.VMEM)],
        out_specs=pl.BlockSpec(memory_space=pltpu.VMEM),
        scratch_shapes=[pltpu.SemaphoreType.DMA((2,)), pltpu.SemaphoreType.DMA((2,))],
        compiler_params=pltpu.CompilerParams(
            collective_id=identity, has_side_effects=True, vmem_limit_bytes=16 << 20
        ),
    )(plane)
    before = jnp.where(me == 0, jnp.zeros_like(plane), got[0])
    after = jnp.where(me == size - 1, jnp.zeros_like(plane), got[1])
    return before, after


def dft_table(length):
    position = jnp.arange(length, dtype=jnp.int32)
    product_mod = position[:, None] * position[None, :] % length
    angles = product_mod.astype(jnp.float32) * (2.0 * math.pi / length)
    norm_scale = 1.0 / math.sqrt(length)
    cosine = jnp.cos(angles) * norm_scale
    sine = jnp.sin(angles) * norm_scale
    upper_half = jnp.stack([cosine, sine], axis=1)
    lower_half = jnp.stack([-sine, cosine], axis=1)
    return jnp.stack([upper_half, lower_half], axis=0).astype(jnp.bfloat16)


def complex_times(maps, values):
    maps_real = maps[0].astype(jnp.float32)
    maps_imag = maps[1].astype(jnp.float32)
    value_real = values[0].astype(jnp.float32)
    value_imag = values[1].astype(jnp.float32)
    return jnp.stack(
        [
            maps_real * value_real - maps_imag * value_imag,
            maps_real * value_imag + maps_imag * value_real,
        ]
    ).astype(jnp.bfloat16)


def conj_summed(maps, values):
    maps_real = maps[0].astype(jnp.float32)
    maps_imag = maps[1].astype(jnp.float32)
    real_part = jnp.sum(maps_real * values[0] + maps_imag * values[1], axis=0)
    imag_part = jnp.sum(maps_real * values[1] - maps_imag * values[0], axis=0)
    return jnp.stack([real_part, imag_part])


def forward_y(table_y, coil_image):
    return jnp.einsum(
        "pkqn,qcabn->pcabk", table_y, coil_image, preferred_element_type=jnp.float32
    ).astype(jnp.bfloat16)


def inverse_y(table_y, back_z):
    return jnp.einsum("qkpn,qcabk->pcabn", table_y, back_z, preferred_element_type=jnp.float32)


def residual_back(table_z, hybrid, measured, sample_gate):
    predicted = jnp.einsum("pkqn,qcnxy->pckxy", table_z, hybrid, preferred_element_type=jnp.float32)
    residual = (sample_gate * (predicted - measured.astype(jnp.float32))).astype(jnp.bfloat16)
    return jnp.einsum(
        "qkpn,qckxy->pcnxy", table_z, residual, preferred_element_type=jnp.float32
    ).astype(jnp.bfloat16)


def plane_conv(values, conv_plane):
    first = lax.conv_general_dilated(
        values,
        conv_plane,
        (1, 1),
        "SAME",
        dimension_numbers=("CNHW", "OIHW", "CNHW"),
        preferred_element_type=jnp.float32,
    )
    return jax.nn.relu(first).astype(jnp.bfloat16)


def denoise(noisy_low, conv_plane, conv_depth, conv_output, identity):
    parts, planes, reads, lines = noisy_low.shape
    flat = noisy_low.reshape(parts, planes * reads, lines)
    before, after = halos(flat[:, :, :], identity)
    wide = jnp.stack([before, flat, after], axis=2).reshape(parts, planes, 3, lines)
    first = lax.conv_general_dilated(
        wide,
        conv_plane,
        (1, 1),
        ((0, 0), (1, 1)),
        dimension_numbers=("CNHW", "OIHW", "CNHW"),
        preferred_element_type=jnp.float32,
    )
    act_one = jax.nn.relu(first).astype(jnp.bfloat16)
    padded = jnp.pad(act_one, ((0, 0), (1, 1), (0, 0), (0, 0)))
    stacked = jnp.concatenate([padded[:, t : t + planes] for t in range(3)], axis=0)
    depth = conv_depth.reshape(conv_depth.shape[0], -1)
    mixed = jnp.einsum("oi,izxy->ozxy", depth, stacked, preferred_element_type=jnp.float32)
    act_two = jax.nn.relu(mixed).astype(jnp.bfloat16)
    return jnp.einsum("pi,izxy->pzxy", conv_output, act_two, preferred_element_type=jnp.float32)


def body(measured, coil_maps, start_image, line_mask, conv_plane, conv_depth, conv_output):
    table_y = dft_table(measured.shape[4])
    table_z = dft_table(measured.shape[2])
    sample_gate = line_mask.astype(jnp.float32)[:, None, :]
    sent = jnp.concatenate([coil_maps, start_image.astype(jnp.bfloat16)[:, None]], axis=1)
    parts, coils, slices, reads, lines = coil_maps.shape
    size = lax.axis_size("slab")
    sent = jnp.moveaxis(sent, 3, 0).reshape(size, -1, lines)
    got = exchange(sent, 1, pl.ANY).reshape(size, parts, coils + 1, slices, lines)
    got = jnp.moveaxis(got, 0, 2).reshape(parts, coils + 1, size * slices, 1, lines)
    maps = got[:, :coils]
    estimate = got[:, coils].astype(jnp.float32)
    for index_pass in range(PASSES):
        image_low = estimate.astype(jnp.bfloat16)
        coil_image = complex_times(maps, image_low[:, None])
        hybrid = forward_y(table_y, coil_image)
        back_z = residual_back(table_z, hybrid, measured, sample_gate)
        back_y = inverse_y(table_y, back_z)
        gradient = conj_summed(maps, back_y)
        noisy_image = estimate - gradient
        estimate = noisy_image + denoise(
            noisy_image.astype(jnp.bfloat16), conv_plane, conv_depth, conv_output, 3 + index_pass
        )
    leave = estimate.astype(jnp.bfloat16).reshape(parts, size, slices, lines)
    leave = jnp.moveaxis(leave, 1, 0).reshape(size, parts * slices, lines)
    out = exchange(leave, 2, pltpu.VMEM).reshape(reads, parts, slices, lines)
    return jnp.transpose(out, (1, 2, 0, 3)).astype(jnp.float32)


def solution(mesh):
    in_specs = (
        P("exam", None, None, "slab", None),
        P("exam", None, "slab", None, None),
        P("exam", "slab", None, None),
        P("exam", None),
        P(),
        P(),
        P(),
    )
    out_specs = P("exam", "slab", None, None)
    return jax.shard_map(body, mesh=mesh, in_specs=in_specs, out_specs=out_specs, check_vma=False)
```

```python
import functools
import math

import jax
import jax.numpy as jnp
import numpy as np
from jax import lax
from jax.experimental import pallas as pl
from jax.experimental.pallas import tpu as pltpu
from jax.sharding import PartitionSpec as P

PASSES = 2


def partner(me, flips):
    other = me
    bit = 1
    while bit <= flips:
        if flips & bit:
            other = other + bit * (1 - 2 * lax.rem(lax.div(me, bit), 2))
        bit *= 2
    return other


def flip_order(size):
    half = size // 2
    order = []
    for low in range(half):
        order.append(half + low)
        if low:
            order.append(low)
    return order


def exchange_kernel(size, sent_ref, got_ref, send_sem, recv_sem, own_sem):
    me = lax.axis_index("slab")
    order = flip_order(size)
    barrier = pltpu.get_barrier_semaphore()
    for flips in order:
        pl.semaphore_signal(barrier, inc=1, device_id={"slab": partner(me, flips)})
    own = pltpu.make_async_copy(sent_ref.at[me], got_ref.at[me], own_sem)
    own.start()
    pl.semaphore_wait(barrier, size - 1)
    copies = []
    for flips in order:
        to = partner(me, flips)
        copy = pltpu.make_async_remote_copy(
            src_ref=sent_ref.at[to],
            dst_ref=got_ref.at[me],
            send_sem=send_sem.at[flips],
            recv_sem=recv_sem.at[flips],
            device_id={"slab": to},
        )
        copy.start()
        copies.append(copy)
    own.wait()
    for copy in copies:
        copy.wait()


def exchange(blocks, identity, space):
    size = blocks.shape[0]
    return pl.pallas_call(
        functools.partial(exchange_kernel, size),
        out_shape=jax.ShapeDtypeStruct(blocks.shape, blocks.dtype),
        in_specs=[pl.BlockSpec(memory_space=space)],
        out_specs=pl.BlockSpec(memory_space=space),
        scratch_shapes=[
            pltpu.SemaphoreType.DMA((size,)),
            pltpu.SemaphoreType.DMA((size,)),
            pltpu.SemaphoreType.DMA,
        ],
        compiler_params=pltpu.CompilerParams(
            collective_id=identity, has_side_effects=True, vmem_limit_bytes=32 << 20
        ),
    )(blocks)


def halo_kernel(size, plane_ref, out_ref, send_sem, recv_sem):
    me = lax.axis_index("slab")
    sides = (lax.rem(me + 1, size), lax.rem(me + size - 1, size))
    barrier = pltpu.get_barrier_semaphore()
    for side in sides:
        pl.semaphore_signal(barrier, inc=1, device_id={"slab": side})
    pl.semaphore_wait(barrier, 2)
    copies = []
    for at, side in enumerate(sides):
        copy = pltpu.make_async_remote_copy(
            src_ref=plane_ref,
            dst_ref=out_ref.at[at],
            send_sem=send_sem.at[at],
            recv_sem=recv_sem.at[at],
            device_id={"slab": side},
        )
        copy.start()
        copies.append(copy)
    for copy in copies:
        copy.wait()


def halos(plane, identity):
    size = lax.axis_size("slab")
    me = lax.axis_index("slab")
    got = pl.pallas_call(
        functools.partial(halo_kernel, size),
        out_shape=jax.ShapeDtypeStruct((2,) + plane.shape, plane.dtype),
        in_specs=[pl.BlockSpec(memory_space=pltpu.VMEM)],
        out_specs=pl.BlockSpec(memory_space=pltpu.VMEM),
        scratch_shapes=[pltpu.SemaphoreType.DMA((2,)), pltpu.SemaphoreType.DMA((2,))],
        compiler_params=pltpu.CompilerParams(
            collective_id=identity, has_side_effects=True, vmem_limit_bytes=16 << 20
        ),
    )(plane)
    keep = jnp.stack([me > 0, me < size - 1]).astype(jnp.float32)
    return got, keep


def dft_parts(length):
    position = np.arange(length)
    angles = (position[:, None] * position[None, :] % length) * (2.0 * math.pi / length)
    scale = 1.0 / math.sqrt(length)
    cosine = (np.cos(angles) * scale).astype(jnp.bfloat16)
    sine = (np.sin(angles) * scale).astype(jnp.bfloat16)
    return cosine, sine


def table_wide(length):
    cosine, sine = dft_parts(length)
    gap = -length % 128
    return np.concatenate([cosine, np.zeros((length, gap), cosine.dtype), sine], axis=1)


def table_square(length):
    cosine, sine = dft_parts(length)
    upper = np.concatenate([cosine, sine], axis=1)
    lower = np.concatenate([-sine, cosine], axis=1)
    return np.concatenate([upper, lower], axis=0)


def dot(left, right):
    return jnp.dot(left, right, preferred_element_type=jnp.float32)


def gradient_kernel(
    maps_ref, measured_ref, gate_ref, image_ref, wide_ref, square_ref, turned_ref,
    noisy_ref, low_ref, total_ref,
):
    step = pl.program_id(0)
    planes, lines = gate_ref.shape
    start = wide_ref.shape[1] - lines
    f32, bf16 = jnp.float32, jnp.bfloat16

    @pl.when(step == 0)
    def _():
        total_ref[...] = jnp.zeros_like(total_ref)

    image_re = image_ref[0].astype(bf16).astype(f32)
    image_im = image_ref[1].astype(bf16).astype(f32)
    gate = gate_ref[...].astype(f32)
    gate = jnp.concatenate([gate, gate], axis=0)
    wide = wide_ref[...]
    for coil in range(maps_ref.shape[1]):
        maps_re = maps_ref[0, coil].astype(f32)
        maps_im = maps_ref[1, coil].astype(f32)
        both = jnp.concatenate(
            [maps_re * image_re - maps_im * image_im, maps_re * image_im + maps_im * image_re],
            axis=0,
        ).astype(bf16)
        out = dot(both, wide)
        cos_part, sin_part = out[:, :lines], out[:, start:]
        hybrid = jnp.concatenate(
            [cos_part[:planes] + sin_part[planes:], cos_part[planes:] - sin_part[:planes]], axis=0
        ).astype(bf16)
        predicted = dot(square_ref[...], hybrid)
        seen = jnp.concatenate([measured_ref[0, coil], measured_ref[1, coil]], axis=0)
        residual = (gate * (predicted - seen.astype(f32))).astype(bf16)
        back_z = dot(turned_ref[...], residual).astype(bf16)
        out = dot(back_z, wide)
        cos_part, sin_part = out[:, :lines], out[:, start:]
        back_re = cos_part[:planes] - sin_part[planes:]
        back_im = cos_part[planes:] + sin_part[:planes]
        total_ref[0] += maps_re * back_re + maps_im * back_im
        total_ref[1] += maps_re * back_im - maps_im * back_re

    @pl.when(step == pl.num_programs(0) - 1)
    def _():
        noisy = image_ref[...] - total_ref[...]
        noisy_ref[...] = noisy
        low_ref[...] = noisy.astype(bf16)


def gradient_step(maps, measured, gate, image, wide, square, turned):
    parts, coils, planes, lines = measured.shape
    group = 2
    whole = lambda shape: pl.BlockSpec(shape, lambda i: (0,) * len(shape))
    by_coil = pl.BlockSpec((parts, group, planes, lines), lambda i: (0, i, 0, 0))
    shape = (parts, planes, lines)
    return pl.pallas_call(
        gradient_kernel,
        grid=(coils // group,),
        in_specs=[by_coil, by_coil, whole(gate.shape), whole(shape)]
        + [whole(t.shape) for t in (wide, square, turned)],
        out_specs=[whole(shape), whole(shape)],
        out_shape=[
            jax.ShapeDtypeStruct(shape, jnp.float32),
            jax.ShapeDtypeStruct(shape, jnp.bfloat16),
        ],
        scratch_shapes=[pltpu.VMEM(shape, jnp.float32)],
        compiler_params=pltpu.CompilerParams(vmem_limit_bytes=40 << 20),
    )(maps, measured, gate, image, wide, square, turned)


GROUP = 8


def denoise_kernel(noisy_ref, low_ref, halo_ref, keep_ref, one_ref, two_ref, three_ref, out_ref, act_ref):
    parts, planes, lines = noisy_ref.shape
    hidden = two_ref.shape[0] // GROUP
    f32, bf16 = jnp.float32, jnp.bfloat16
    edge = jnp.zeros((planes, 1), f32)
    taps = []
    for read in range(3):
        for part in range(parts):
            if read == 1:
                plane = low_ref[part].astype(f32)
            else:
                side = read // 2
                plane = halo_ref[side, part].astype(f32) * keep_ref[side]
            taps.append(jnp.concatenate([edge, plane[:, :-1]], axis=1))
            taps.append(plane)
            taps.append(jnp.concatenate([plane[:, 1:], edge], axis=1))
    act_ref[:hidden] = jnp.zeros((hidden, lines), bf16)
    act_ref[(planes + 1) * hidden :] = jnp.zeros((hidden, lines), bf16)
    rows = GROUP * hidden
    for z in range(0, planes, GROUP):
        patch = jnp.concatenate([tap[z : z + GROUP] for tap in taps], axis=0).astype(bf16)
        first = dot(one_ref[...], patch)
        at = (z + 1) * hidden
        act_ref[at : at + rows] = jnp.maximum(first, 0.0).astype(bf16)
    for z in range(0, planes, GROUP):
        window = act_ref[z * hidden : (z + GROUP + 2) * hidden]
        second = jnp.maximum(dot(two_ref[...], window), 0.0).astype(bf16)
        last = dot(three_ref[...], second)
        for part in range(parts):
            add = last[part * GROUP : (part + 1) * GROUP]
            out_ref[part, z : z + GROUP] = noisy_ref[part, z : z + GROUP] + add


def denoise_weights(conv_plane, conv_depth, conv_output):
    hidden, parts = conv_plane.shape[:2]
    eye = np.eye(GROUP, dtype=np.float32).astype(jnp.bfloat16)
    taps = jnp.transpose(conv_plane, (0, 2, 1, 3)).reshape(hidden, -1)
    one = eye[:, None, None, :] * taps[None, :, :, None]
    one = one.reshape(GROUP * hidden, -1)
    shifts = np.stack([np.eye(GROUP, GROUP + 2, t, np.float32) for t in range(3)])
    shifts = shifts.astype(jnp.bfloat16)
    two = sum(shifts[t][:, None, :, None] * conv_depth[:, t, :][None, :, None, :] for t in range(3))
    two = two.reshape(GROUP * hidden, -1)
    three = eye[None, :, :, None] * conv_output[:, None, None, :]
    three = three.reshape(parts * GROUP, -1)
    return one, two, three


def denoise(noisy, low, weights, identity):
    got, keep = halos(low, identity)
    parts, planes, lines = noisy.shape
    hidden = weights[1].shape[0] // GROUP
    vmem = pl.BlockSpec(memory_space=pltpu.VMEM)
    return pl.pallas_call(
        denoise_kernel,
        out_shape=jax.ShapeDtypeStruct(noisy.shape, jnp.float32),
        in_specs=[vmem] * 3 + [pl.BlockSpec(memory_space=pltpu.SMEM)] + [vmem] * 3,
        out_specs=vmem,
        scratch_shapes=[pltpu.VMEM(((planes + 2) * hidden, lines), jnp.bfloat16)],
        compiler_params=pltpu.CompilerParams(vmem_limit_bytes=40 << 20),
    )(noisy, low, got, keep, *weights)


def body(measured, coil_maps, start_image, line_mask, conv_plane, conv_depth, conv_output):
    parts, coils, slices, reads, lines = coil_maps.shape
    size = lax.axis_size("slab")
    wide = jnp.asarray(table_wide(lines))
    square = table_square(slices * size)
    square, turned = jnp.asarray(square), jnp.asarray(square.T)
    weights = denoise_weights(conv_plane, conv_depth, conv_output)
    sent = jnp.concatenate([coil_maps, start_image.astype(jnp.bfloat16)[:, None]], axis=1)
    sent = jnp.moveaxis(sent, 3, 0).reshape(size, -1, lines)
    got = exchange(sent, 1, pl.ANY).reshape(size, parts, coils + 1, slices, lines)
    maps = jnp.moveaxis(got, 0, 2).reshape(parts, coils + 1, size * slices, lines)
    estimate = maps[:, coils].astype(jnp.float32)
    seen = measured.reshape(parts, coils, size * slices, lines)
    for index_pass in range(PASSES):
        noisy, low = gradient_step(maps, seen, line_mask, estimate, wide, square, turned)
        estimate = denoise(noisy, low, weights, 3 + index_pass)
    leave = estimate.astype(jnp.bfloat16).reshape(parts, size, slices, lines)
    leave = jnp.moveaxis(leave, 1, 0).reshape(size, parts * slices, lines)
    out = exchange(leave, 2, pltpu.VMEM).reshape(reads, parts, slices, lines)
    return jnp.transpose(out, (1, 2, 0, 3)).astype(jnp.float32)


def solution(mesh):
    in_specs = (
        P("exam", None, None, "slab", None),
        P("exam", None, "slab", None, None),
        P("exam", "slab", None, None),
        P("exam", None),
        P(),
        P(),
        P(),
    )
    out_specs = P("exam", "slab", None, None)
    return jax.shard_map(body, mesh=mesh, in_specs=in_specs, out_specs=out_specs, check_vma=False)
```

```python
import functools
import math

import jax
import jax.numpy as jnp
import numpy as np
from jax import lax
from jax.experimental import pallas as pl
from jax.experimental.pallas import tpu as pltpu
from jax.sharding import PartitionSpec as P

PASSES = 2


def partner(me, flips):
    other = me
    bit = 1
    while bit <= flips:
        if flips & bit:
            other = other + bit * (1 - 2 * lax.rem(lax.div(me, bit), 2))
        bit *= 2
    return other


def flip_order(size):
    half = size // 2
    order = []
    for low in range(half):
        order.append(half + low)
        if low:
            order.append(low)
    return order


def exchange_kernel(size, sent_ref, got_ref, send_sem, recv_sem, own_sem):
    me = lax.axis_index("slab")
    order = flip_order(size)
    barrier = pltpu.get_barrier_semaphore()
    for flips in order:
        pl.semaphore_signal(barrier, inc=1, device_id={"slab": partner(me, flips)})
    own = pltpu.make_async_copy(sent_ref.at[me], got_ref.at[me], own_sem)
    own.start()
    pl.semaphore_wait(barrier, size - 1)
    copies = []
    for flips in order:
        to = partner(me, flips)
        copy = pltpu.make_async_remote_copy(
            src_ref=sent_ref.at[to],
            dst_ref=got_ref.at[me],
            send_sem=send_sem.at[flips],
            recv_sem=recv_sem.at[flips],
            device_id={"slab": to},
        )
        copy.start()
        copies.append(copy)
    own.wait()
    for copy in copies:
        copy.wait()


def exchange(blocks, identity, space):
    size = blocks.shape[0]
    return pl.pallas_call(
        functools.partial(exchange_kernel, size),
        out_shape=jax.ShapeDtypeStruct(blocks.shape, blocks.dtype),
        in_specs=[pl.BlockSpec(memory_space=space)],
        out_specs=pl.BlockSpec(memory_space=space),
        scratch_shapes=[
            pltpu.SemaphoreType.DMA((size,)),
            pltpu.SemaphoreType.DMA((size,)),
            pltpu.SemaphoreType.DMA,
        ],
        compiler_params=pltpu.CompilerParams(
            collective_id=identity, has_side_effects=True, vmem_limit_bytes=32 << 20
        ),
    )(blocks)


def halo_kernel(size, plane_ref, out_ref, send_sem, recv_sem):
    me = lax.axis_index("slab")
    barrier = pltpu.get_barrier_semaphore()
    copies = []
    for at, step in enumerate((1, -1)):
        side = lax.rem(me + step + size, size)
        copies.append(
            pltpu.make_async_remote_copy(
                src_ref=plane_ref,
                dst_ref=out_ref.at[at],
                send_sem=send_sem.at[at],
                recv_sem=recv_sem.at[at],
                device_id={"slab": side},
            )
        )
    has = (me < size - 1, me > 0)
    for at, step in enumerate((1, -1)):

        @pl.when(has[at])
        def _():
            side = lax.rem(me + step + size, size)
            pl.semaphore_signal(barrier, inc=1, device_id={"slab": side})

    pl.semaphore_wait(barrier, has[0].astype(jnp.int32) + has[1].astype(jnp.int32))

    for at in range(2):

        @pl.when(has[at])
        def _():
            copies[at].start()

    for at in range(2):

        @pl.when(jnp.logical_not(has[1 - at]))
        def _():
            out_ref[at] = jnp.zeros(out_ref.shape[1:], out_ref.dtype)

        @pl.when(has[1 - at])
        def _():
            copies[at].wait_recv()

        @pl.when(has[at])
        def _():
            copies[at].wait_send()


def halos(plane, identity):
    size = lax.axis_size("slab")
    return pl.pallas_call(
        functools.partial(halo_kernel, size),
        out_shape=jax.ShapeDtypeStruct((2,) + plane.shape, plane.dtype),
        in_specs=[pl.BlockSpec(memory_space=pltpu.VMEM)],
        out_specs=pl.BlockSpec(memory_space=pltpu.VMEM),
        scratch_shapes=[pltpu.SemaphoreType.DMA((2,)), pltpu.SemaphoreType.DMA((2,))],
        compiler_params=pltpu.CompilerParams(
            collective_id=identity, has_side_effects=True, vmem_limit_bytes=16 << 20
        ),
    )(plane)


def dft_parts(length):
    position = np.arange(length)
    angles = (position[:, None] * position[None, :] % length) * (2.0 * math.pi / length)
    scale = 1.0 / math.sqrt(length)
    cosine = (np.cos(angles) * scale).astype(jnp.bfloat16)
    sine = (np.sin(angles) * scale).astype(jnp.bfloat16)
    return cosine, sine


def table_wide(length):
    cosine, sine = dft_parts(length)
    gap = -length % 128
    return np.concatenate([cosine, np.zeros((length, gap), cosine.dtype), sine], axis=1)


def table_square(length):
    cosine, sine = dft_parts(length)
    upper = np.concatenate([cosine, sine], axis=1)
    lower = np.concatenate([-sine, cosine], axis=1)
    return np.concatenate([upper, lower], axis=0)


def dot(left, right):
    return jnp.dot(left, right, preferred_element_type=jnp.float32)


def gradient_kernel(
    maps_ref, measured_ref, gate_ref, image_ref, wide_ref, square_ref, turned_ref,
    noisy_ref, low_ref, total_ref,
):
    step = pl.program_id(0)
    planes, lines = gate_ref.shape
    start = wide_ref.shape[1] - lines
    f32, bf16 = jnp.float32, jnp.bfloat16

    @pl.when(step == 0)
    def _():
        total_ref[...] = jnp.zeros_like(total_ref)

    image_re = image_ref[0].astype(bf16).astype(f32)
    image_im = image_ref[1].astype(bf16).astype(f32)
    gate = gate_ref[...].astype(f32)
    gate = jnp.concatenate([gate, gate], axis=0)
    wide = wide_ref[...]
    coils = maps_ref.shape[1]
    rows = 2 * planes
    both = []
    for coil in range(coils):
        maps_re = maps_ref[0, coil].astype(f32)
        maps_im = maps_ref[1, coil].astype(f32)
        both.append((maps_re * image_re - maps_im * image_im).astype(bf16))
        both.append((maps_re * image_im + maps_im * image_re).astype(bf16))
    forward = dot(jnp.concatenate(both, axis=0), wide)
    back = []
    for coil in range(coils):
        out = forward[coil * rows : (coil + 1) * rows]
        cos_part, sin_part = out[:, :lines], out[:, start:]
        hybrid = jnp.concatenate(
            [cos_part[:planes] + sin_part[planes:], cos_part[planes:] - sin_part[:planes]], axis=0
        ).astype(bf16)
        predicted = dot(square_ref[...], hybrid)
        seen = jnp.concatenate([measured_ref[0, coil], measured_ref[1, coil]], axis=0)
        residual = (gate * (predicted - seen.astype(f32))).astype(bf16)
        back.append(dot(turned_ref[...], residual).astype(bf16))
    inverse = dot(jnp.concatenate(back, axis=0), wide)
    sum_re = total_ref[0]
    sum_im = total_ref[1]
    for coil in range(coils):
        maps_re = maps_ref[0, coil].astype(f32)
        maps_im = maps_ref[1, coil].astype(f32)
        out = inverse[coil * rows : (coil + 1) * rows]
        cos_part, sin_part = out[:, :lines], out[:, start:]
        back_re = cos_part[:planes] - sin_part[planes:]
        back_im = cos_part[planes:] + sin_part[:planes]
        sum_re += maps_re * back_re + maps_im * back_im
        sum_im += maps_re * back_im - maps_im * back_re
    total_ref[0] = sum_re
    total_ref[1] = sum_im

    @pl.when(step == pl.num_programs(0) - 1)
    def _():
        noisy = image_ref[...] - total_ref[...]
        noisy_ref[...] = noisy
        low_ref[...] = noisy.astype(bf16)


def gradient_step(maps, measured, gate, image, wide, square, turned):
    parts, coils, planes, lines = measured.shape
    group = math.gcd(coils, 4)
    whole = lambda shape: pl.BlockSpec(shape, lambda i: (0,) * len(shape))
    by_coil = pl.BlockSpec((parts, group, planes, lines), lambda i: (0, i, 0, 0))
    shape = (parts, planes, lines)
    return pl.pallas_call(
        gradient_kernel,
        grid=(coils // group,),
        in_specs=[by_coil, by_coil, whole(gate.shape), whole(shape)]
        + [whole(t.shape) for t in (wide, square, turned)],
        out_specs=[whole(shape), whole(shape)],
        out_shape=[
            jax.ShapeDtypeStruct(shape, jnp.float32),
            jax.ShapeDtypeStruct(shape, jnp.bfloat16),
        ],
        scratch_shapes=[pltpu.VMEM(shape, jnp.float32)],
        compiler_params=pltpu.CompilerParams(vmem_limit_bytes=58 << 20),
    )(maps, measured, gate, image, wide, square, turned)


GROUP = 8


def spots(shape):
    return lax.broadcasted_iota(jnp.int32, shape, 0), lax.broadcasted_iota(jnp.int32, shape, 1)


def chosen(condition):
    return jnp.where(condition, 1.0, 0.0).astype(jnp.bfloat16)


def plane_weights(plane):
    hidden, taps = plane.shape
    bits, group_bits = hidden.bit_length() - 1, GROUP.bit_length() - 1
    row, col = spots((taps, taps * GROUP))
    spread = dot(jnp.concatenate([plane] * GROUP, axis=0), chosen(row == (col >> group_bits)))
    row, col = spots(spread.shape)
    return jnp.where((row >> bits) == (col & (GROUP - 1)), spread, 0.0).astype(jnp.bfloat16)


def depth_weights(depth):
    hidden, taps = depth.shape
    bits = hidden.bit_length() - 1
    tall = jnp.concatenate([depth] * GROUP, axis=0)
    total = jnp.zeros((GROUP * hidden, (GROUP + 2) * hidden), jnp.float32)
    for t in range(3):
        row, col = spots((taps, total.shape[1]))
        spread = dot(tall, chosen(row == (col & (hidden - 1)) + t * hidden))
        row, col = spots(total.shape)
        total = jnp.where((col >> bits) - (row >> bits) == t, spread, total)
    return total.astype(jnp.bfloat16)


def output_weights(output):
    parts, hidden = output.shape
    bits = hidden.bit_length() - 1
    wide = output.astype(jnp.float32)
    tall = jnp.concatenate(
        [jnp.broadcast_to(wide[p : p + 1], (GROUP, hidden)) for p in range(parts)], axis=0
    ).astype(jnp.bfloat16)
    row, col = spots((hidden, GROUP * hidden))
    spread = dot(tall, chosen(row == (col & (hidden - 1))))
    row, col = spots(spread.shape)
    return jnp.where((row & (GROUP - 1)) == (col >> bits), spread, 0.0).astype(jnp.bfloat16)


def denoise_kernel(noisy_ref, low_ref, halo_ref, plane_ref, depth_ref, output_ref, out_ref, act_ref):
    parts, planes, lines = noisy_ref.shape
    hidden = depth_ref.shape[0]
    f32, bf16 = jnp.float32, jnp.bfloat16
    one = plane_weights(plane_ref[...])
    two = depth_weights(depth_ref[...])
    three = output_weights(output_ref[...])
    edge = jnp.zeros((planes, 1), f32)
    taps = []
    for part in range(parts):
        for plane in (halo_ref[0, part], low_ref[part], halo_ref[1, part]):
            plane = plane.astype(f32)
            taps.append(jnp.concatenate([edge, plane[:, :-1]], axis=1))
            taps.append(plane)
            taps.append(jnp.concatenate([plane[:, 1:], edge], axis=1))
    act_ref[:hidden] = jnp.zeros((hidden, lines), bf16)
    act_ref[(planes + 1) * hidden :] = jnp.zeros((hidden, lines), bf16)
    rows = GROUP * hidden
    for z in range(0, planes, GROUP):
        patch = jnp.concatenate([tap[z : z + GROUP] for tap in taps], axis=0).astype(bf16)
        first = dot(one, patch)
        at = (z + 1) * hidden
        act_ref[at : at + rows] = jnp.maximum(first, 0.0).astype(bf16)
    for z in range(0, planes, GROUP):
        window = act_ref[z * hidden : (z + GROUP + 2) * hidden]
        second = jnp.maximum(dot(two, window), 0.0).astype(bf16)
        last = dot(three, second)
        for part in range(parts):
            add = last[part * GROUP : (part + 1) * GROUP]
            out_ref[part, z : z + GROUP] = noisy_ref[part, z : z + GROUP] + add


def denoise(noisy, low, weights, identity):
    got = halos(low, identity)
    parts, planes, lines = noisy.shape
    hidden = weights[1].shape[0]
    vmem = pl.BlockSpec(memory_space=pltpu.VMEM)
    return pl.pallas_call(
        denoise_kernel,
        out_shape=jax.ShapeDtypeStruct(noisy.shape, jnp.float32),
        in_specs=[vmem] * 6,
        out_specs=vmem,
        scratch_shapes=[pltpu.VMEM(((planes + 2) * hidden, lines), jnp.bfloat16)],
        compiler_params=pltpu.CompilerParams(vmem_limit_bytes=40 << 20),
    )(noisy, low, got, *weights)


def body(measured, coil_maps, start_image, line_mask, conv_plane, conv_depth, conv_output):
    parts, coils, slices, reads, lines = coil_maps.shape
    size = lax.axis_size("slab")
    wide = jnp.asarray(table_wide(lines))
    square = table_square(slices * size)
    square, turned = jnp.asarray(square), jnp.asarray(square.T)
    hidden = conv_plane.shape[0]
    weights = (conv_plane.reshape(hidden, -1), conv_depth.reshape(hidden, -1), conv_output)
    sent = jnp.concatenate([coil_maps, start_image.astype(jnp.bfloat16)[:, None]], axis=1)
    sent = jnp.moveaxis(sent, 3, 0).reshape(size, -1, lines)
    got = exchange(sent, 1, pl.ANY).reshape(size, parts, coils + 1, slices, lines)
    maps = jnp.moveaxis(got, 0, 2).reshape(parts, coils + 1, size * slices, lines)
    estimate = maps[:, coils].astype(jnp.float32)
    seen = measured.reshape(parts, coils, size * slices, lines)
    for index_pass in range(PASSES):
        noisy, low = gradient_step(maps, seen, line_mask, estimate, wide, square, turned)
        estimate = denoise(noisy, low, weights, 3 + index_pass)
    leave = estimate.astype(jnp.bfloat16).reshape(parts, size, slices, lines)
    leave = jnp.moveaxis(leave, 1, 0).reshape(size, parts * slices, lines)
    out = exchange(leave, 2, pltpu.VMEM).reshape(reads, parts, slices, lines)
    return jnp.transpose(out, (1, 2, 0, 3)).astype(jnp.float32)


def solution(mesh):
    in_specs = (
        P("exam", None, None, "slab", None),
        P("exam", None, "slab", None, None),
        P("exam", "slab", None, None),
        P("exam", None),
        P(),
        P(),
        P(),
    )
    out_specs = P("exam", "slab", None, None)
    return jax.shard_map(body, mesh=mesh, in_specs=in_specs, out_specs=out_specs, check_vma=False)
```

```python
import functools
import math

import jax
import jax.numpy as jnp
import numpy as np
from jax import lax
from jax.experimental import pallas as pl
from jax.experimental.pallas import tpu as pltpu
from jax.sharding import PartitionSpec as P

PASSES = 2


def partner(me, flips):
    other = me
    bit = 1
    while bit <= flips:
        if flips & bit:
            other = other + bit * (1 - 2 * lax.rem(lax.div(me, bit), 2))
        bit *= 2
    return other


def flip_order(size):
    half = size // 2
    order = []
    for low in range(half):
        order.append(half + low)
        if low:
            order.append(low)
    return order


def exchange_kernel(size, sent_ref, got_ref, send_sem, recv_sem, own_sem):
    me = lax.axis_index("slab")
    order = flip_order(size)
    barrier = pltpu.get_barrier_semaphore()
    for flips in order:
        pl.semaphore_signal(barrier, inc=1, device_id={"slab": partner(me, flips)})
    own = pltpu.make_async_copy(sent_ref.at[me], got_ref.at[me], own_sem)
    own.start()
    pl.semaphore_wait(barrier, size - 1)
    copies = []
    for flips in order:
        to = partner(me, flips)
        copy = pltpu.make_async_remote_copy(
            src_ref=sent_ref.at[to],
            dst_ref=got_ref.at[me],
            send_sem=send_sem.at[flips],
            recv_sem=recv_sem.at[flips],
            device_id={"slab": to},
        )
        copy.start()
        copies.append(copy)
    own.wait()
    for copy in copies:
        copy.wait()


def exchange(blocks, identity, space):
    size = blocks.shape[0]
    return pl.pallas_call(
        functools.partial(exchange_kernel, size),
        out_shape=jax.ShapeDtypeStruct(blocks.shape, blocks.dtype),
        in_specs=[pl.BlockSpec(memory_space=space)],
        out_specs=pl.BlockSpec(memory_space=space),
        scratch_shapes=[
            pltpu.SemaphoreType.DMA((size,)),
            pltpu.SemaphoreType.DMA((size,)),
            pltpu.SemaphoreType.DMA,
        ],
        compiler_params=pltpu.CompilerParams(
            collective_id=identity, has_side_effects=True, vmem_limit_bytes=32 << 20
        ),
    )(blocks)


def halo_kernel(size, plane_ref, out_ref, send_sem, recv_sem):
    me = lax.axis_index("slab")
    barrier = pltpu.get_barrier_semaphore()
    copies = []
    for at, step in enumerate((1, -1)):
        side = lax.rem(me + step + size, size)
        copies.append(
            pltpu.make_async_remote_copy(
                src_ref=plane_ref,
                dst_ref=out_ref.at[at],
                send_sem=send_sem.at[at],
                recv_sem=recv_sem.at[at],
                device_id={"slab": side},
            )
        )
    has = (me < size - 1, me > 0)
    for at, step in enumerate((1, -1)):

        @pl.when(has[at])
        def _():
            side = lax.rem(me + step + size, size)
            pl.semaphore_signal(barrier, inc=1, device_id={"slab": side})

    pl.semaphore_wait(barrier, has[0].astype(jnp.int32) + has[1].astype(jnp.int32))

    for at in range(2):

        @pl.when(has[at])
        def _():
            copies[at].start()

    for at in range(2):

        @pl.when(jnp.logical_not(has[1 - at]))
        def _():
            out_ref[at] = jnp.zeros(out_ref.shape[1:], out_ref.dtype)

        @pl.when(has[1 - at])
        def _():
            copies[at].wait_recv()

        @pl.when(has[at])
        def _():
            copies[at].wait_send()


def halos(plane, identity):
    size = lax.axis_size("slab")
    return pl.pallas_call(
        functools.partial(halo_kernel, size),
        out_shape=jax.ShapeDtypeStruct((2,) + plane.shape, plane.dtype),
        in_specs=[pl.BlockSpec(memory_space=pltpu.VMEM)],
        out_specs=pl.BlockSpec(memory_space=pltpu.VMEM),
        scratch_shapes=[pltpu.SemaphoreType.DMA((2,)), pltpu.SemaphoreType.DMA((2,))],
        compiler_params=pltpu.CompilerParams(
            collective_id=identity, has_side_effects=True, vmem_limit_bytes=16 << 20
        ),
    )(plane)


def dft_parts(length):
    position = np.arange(length)
    angles = (position[:, None] * position[None, :] % length) * (2.0 * math.pi / length)
    scale = 1.0 / math.sqrt(length)
    cosine = (np.cos(angles) * scale).astype(jnp.bfloat16)
    sine = (np.sin(angles) * scale).astype(jnp.bfloat16)
    return cosine, sine


def table_wide(length):
    cosine, sine = dft_parts(length)
    gap = -length % 128
    return np.concatenate([cosine, np.zeros((length, gap), cosine.dtype), sine], axis=1)


def table_square(length):
    cosine, sine = dft_parts(length)
    upper = np.concatenate([cosine, sine], axis=1)
    lower = np.concatenate([-sine, cosine], axis=1)
    return np.concatenate([upper, lower], axis=0)


def dot(left, right):
    return jnp.dot(left, right, preferred_element_type=jnp.float32)


def gradient_kernel(
    maps_ref, measured_ref, gate_ref, image_ref, wide_ref, square_ref, turned_ref,
    noisy_ref, low_ref, total_ref,
):
    step = pl.program_id(0)
    planes, lines = gate_ref.shape
    start = wide_ref.shape[1] - lines
    f32, bf16 = jnp.float32, jnp.bfloat16

    @pl.when(step == 0)
    def _():
        total_ref[...] = jnp.zeros_like(total_ref)

    image_re = image_ref[0].astype(bf16).astype(f32)
    image_im = image_ref[1].astype(bf16).astype(f32)
    gate = gate_ref[...].astype(f32)
    gate = jnp.concatenate([gate, gate], axis=0)
    wide = wide_ref[...]
    coils = maps_ref.shape[1]
    rows = 2 * planes
    both = []
    for coil in range(coils):
        maps_re = maps_ref[0, coil].astype(f32)
        maps_im = maps_ref[1, coil].astype(f32)
        both.append((maps_re * image_re - maps_im * image_im).astype(bf16))
        both.append((maps_re * image_im + maps_im * image_re).astype(bf16))
    forward = dot(jnp.concatenate(both, axis=0), wide)
    back = []
    for coil in range(coils):
        out = forward[coil * rows : (coil + 1) * rows]
        cos_part, sin_part = out[:, :lines], out[:, start:]
        hybrid = jnp.concatenate(
            [cos_part[:planes] + sin_part[planes:], cos_part[planes:] - sin_part[:planes]], axis=0
        ).astype(bf16)
        predicted = dot(square_ref[...], hybrid)
        seen = jnp.concatenate([measured_ref[0, coil], measured_ref[1, coil]], axis=0)
        residual = (gate * (predicted - seen.astype(f32))).astype(bf16)
        back.append(dot(turned_ref[...], residual).astype(bf16))
    inverse = dot(jnp.concatenate(back, axis=0), wide)
    sum_re = total_ref[0]
    sum_im = total_ref[1]
    for coil in range(coils):
        maps_re = maps_ref[0, coil].astype(f32)
        maps_im = maps_ref[1, coil].astype(f32)
        out = inverse[coil * rows : (coil + 1) * rows]
        cos_part, sin_part = out[:, :lines], out[:, start:]
        back_re = cos_part[:planes] - sin_part[planes:]
        back_im = cos_part[planes:] + sin_part[:planes]
        sum_re += maps_re * back_re + maps_im * back_im
        sum_im += maps_re * back_im - maps_im * back_re
    total_ref[0] = sum_re
    total_ref[1] = sum_im

    @pl.when(step == pl.num_programs(0) - 1)
    def _():
        noisy = image_ref[...] - total_ref[...]
        noisy_ref[...] = noisy
        low_ref[...] = noisy.astype(bf16)


def gradient_step(maps, measured, gate, image, wide, square, turned):
    parts, coils, planes, lines = measured.shape
    group = math.gcd(coils, 8)
    whole = lambda shape: pl.BlockSpec(shape, lambda i: (0,) * len(shape))
    by_coil = pl.BlockSpec((parts, group, planes, lines), lambda i: (0, i, 0, 0))
    shape = (parts, planes, lines)
    return pl.pallas_call(
        gradient_kernel,
        grid=(coils // group,),
        in_specs=[by_coil, by_coil, whole(gate.shape), whole(shape)]
        + [whole(t.shape) for t in (wide, square, turned)],
        out_specs=[whole(shape), whole(shape)],
        out_shape=[
            jax.ShapeDtypeStruct(shape, jnp.float32),
            jax.ShapeDtypeStruct(shape, jnp.bfloat16),
        ],
        scratch_shapes=[pltpu.VMEM(shape, jnp.float32)],
        compiler_params=pltpu.CompilerParams(vmem_limit_bytes=58 << 20),
    )(maps, measured, gate, image, wide, square, turned)


GROUP = 8


def spots(shape):
    return lax.broadcasted_iota(jnp.int32, shape, 0), lax.broadcasted_iota(jnp.int32, shape, 1)


def chosen(condition):
    return jnp.where(condition, 1.0, 0.0).astype(jnp.bfloat16)


def plane_weights(plane):
    hidden, taps = plane.shape
    bits, group_bits = hidden.bit_length() - 1, GROUP.bit_length() - 1
    row, col = spots((taps, taps * GROUP))
    spread = dot(jnp.concatenate([plane] * GROUP, axis=0), chosen(row == (col >> group_bits)))
    row, col = spots(spread.shape)
    return jnp.where((row >> bits) == (col & (GROUP - 1)), spread, 0.0).astype(jnp.bfloat16)


def depth_weights(depth):
    hidden, taps = depth.shape
    bits = hidden.bit_length() - 1
    tall = jnp.concatenate([depth] * GROUP, axis=0)
    total = jnp.zeros((GROUP * hidden, (GROUP + 2) * hidden), jnp.float32)
    for t in range(3):
        row, col = spots((taps, total.shape[1]))
        spread = dot(tall, chosen(row == (col & (hidden - 1)) + t * hidden))
        row, col = spots(total.shape)
        total = jnp.where((col >> bits) - (row >> bits) == t, spread, total)
    return total.astype(jnp.bfloat16)


def output_weights(output):
    parts, hidden = output.shape
    bits = hidden.bit_length() - 1
    wide = output.astype(jnp.float32)
    tall = jnp.concatenate(
        [jnp.broadcast_to(wide[p : p + 1], (GROUP, hidden)) for p in range(parts)], axis=0
    ).astype(jnp.bfloat16)
    row, col = spots((hidden, GROUP * hidden))
    spread = dot(tall, chosen(row == (col & (hidden - 1))))
    row, col = spots(spread.shape)
    return jnp.where((row & (GROUP - 1)) == (col >> bits), spread, 0.0).astype(jnp.bfloat16)


def denoise_kernel(noisy_ref, low_ref, halo_ref, plane_ref, depth_ref, output_ref, out_ref, act_ref):
    parts, planes, lines = noisy_ref.shape
    hidden = depth_ref.shape[0]
    f32, bf16 = jnp.float32, jnp.bfloat16
    one = plane_weights(plane_ref[...])
    two = depth_weights(depth_ref[...])
    three = output_weights(output_ref[...])
    edge = jnp.zeros((planes, 1), f32)
    taps = []
    for part in range(parts):
        for plane in (halo_ref[0, part], low_ref[part], halo_ref[1, part]):
            plane = plane.astype(f32)
            taps.append(jnp.concatenate([edge, plane[:, :-1]], axis=1))
            taps.append(plane)
            taps.append(jnp.concatenate([plane[:, 1:], edge], axis=1))
    act_ref[:hidden] = jnp.zeros((hidden, lines), bf16)
    act_ref[(planes + 1) * hidden :] = jnp.zeros((hidden, lines), bf16)
    rows = GROUP * hidden
    for z in range(0, planes, GROUP):
        patch = jnp.concatenate([tap[z : z + GROUP] for tap in taps], axis=0).astype(bf16)
        first = dot(one, patch)
        at = (z + 1) * hidden
        act_ref[at : at + rows] = jnp.maximum(first, 0.0).astype(bf16)
    for z in range(0, planes, GROUP):
        window = act_ref[z * hidden : (z + GROUP + 2) * hidden]
        second = jnp.maximum(dot(two, window), 0.0).astype(bf16)
        last = dot(three, second)
        for part in range(parts):
            add = last[part * GROUP : (part + 1) * GROUP]
            out_ref[part, z : z + GROUP] = noisy_ref[part, z : z + GROUP] + add


def denoise(noisy, low, weights, identity):
    got = halos(low, identity)
    parts, planes, lines = noisy.shape
    hidden = weights[1].shape[0]
    vmem = pl.BlockSpec(memory_space=pltpu.VMEM)
    return pl.pallas_call(
        denoise_kernel,
        out_shape=jax.ShapeDtypeStruct(noisy.shape, jnp.float32),
        in_specs=[vmem] * 6,
        out_specs=vmem,
        scratch_shapes=[pltpu.VMEM(((planes + 2) * hidden, lines), jnp.bfloat16)],
        compiler_params=pltpu.CompilerParams(vmem_limit_bytes=40 << 20),
    )(noisy, low, got, *weights)


def body(measured, coil_maps, start_image, line_mask, conv_plane, conv_depth, conv_output):
    parts, coils, slices, reads, lines = coil_maps.shape
    size = lax.axis_size("slab")
    wide = jnp.asarray(table_wide(lines))
    square = table_square(slices * size)
    square, turned = jnp.asarray(square), jnp.asarray(square.T)
    hidden = conv_plane.shape[0]
    weights = (conv_plane.reshape(hidden, -1), conv_depth.reshape(hidden, -1), conv_output)
    sent = jnp.concatenate([coil_maps, start_image.astype(jnp.bfloat16)[:, None]], axis=1)
    sent = jnp.moveaxis(sent, 3, 0).reshape(size, -1, lines)
    got = exchange(sent, 1, pl.ANY).reshape(size, parts, coils + 1, slices, lines)
    maps = jnp.moveaxis(got, 0, 2).reshape(parts, coils + 1, size * slices, lines)
    estimate = maps[:, coils].astype(jnp.float32)
    seen = measured.reshape(parts, coils, size * slices, lines)
    for index_pass in range(PASSES):
        noisy, low = gradient_step(maps, seen, line_mask, estimate, wide, square, turned)
        estimate = denoise(noisy, low, weights, 3 + index_pass)
    leave = estimate.astype(jnp.bfloat16).reshape(parts, size, slices, lines)
    leave = jnp.moveaxis(leave, 1, 0).reshape(size, parts * slices, lines)
    out = exchange(leave, 2, pltpu.VMEM).reshape(reads, parts, slices, lines)
    return jnp.transpose(out, (1, 2, 0, 3)).astype(jnp.float32)


def solution(mesh):
    in_specs = (
        P("exam", None, None, "slab", None),
        P("exam", None, "slab", None, None),
        P("exam", "slab", None, None),
        P("exam", None),
        P(),
        P(),
        P(),
    )
    out_specs = P("exam", "slab", None, None)
    return jax.shard_map(body, mesh=mesh, in_specs=in_specs, out_specs=out_specs, check_vma=False)
```
